32 devices in a mesh: row: 4 (over y, x), col: 8 (over z, core).
Axes of the slice: x: 2, y: 2, z: 4, core: 2. Of those that a mesh axis runs over, the one named last changes fastest.
Arguments:
- trailing: float32 [10, 4, 256, 5, 8, 256], P(None, 'row', None, None, 'col'), as said below
Outputs:
- factored: float32 [10, 4, 256, 5, 8, 256], P(None, 'row', None, None, 'col')
Inputs may be any that keep to these rules, and one draw needn't show every extreme that they name: trailing is a covariance matrix of points in the plane: symmetric and positive definite, with a nugget added to its diagonal.
All inputs are finite; a program needn't handle non-finite values.
Results may differ from the reference program's by a relative error of at most 0.0041.
Values may be sent and summed in bfloat16 or wider, within the bound.
A program may use at most 128 MiB of HBM per device.

```python
import math
import jax
import jax.numpy as jnp
from jax import lax

PANEL = 256
PANELS = 2
NBLK = 40
N_ROW = 4
N_COL = 8


def draw_trailing(key, part):
    key = jax.random.fold_in(key, 7)
    first_key = jax.random.fold_in(key, 0)
    order_total = NBLK * PANEL
    points = jax.random.uniform(first_key, (order_total, 2), jnp.float32)
    length_scale = 0.2
    across = points[:, 0][:, None] - points[:, 0][None, :]
    along = points[:, 1][:, None] - points[:, 1][None, :]
    scaled = jnp.sqrt(across * across + along * along) * (math.sqrt(3.0) / length_scale)
    kernel = (1.0 + scaled) * jnp.exp(-scaled)
    indices = jnp.arange(order_total)
    kernel = jnp.where(indices[:, None] == indices[None, :], kernel + 0.5, kernel)
    return kernel.reshape(NBLK // N_ROW, N_ROW, PANEL, NBLK // N_COL, N_COL, PANEL)


def setup_inputs(seed: int = 0) -> dict:
    seeds = jax.random.split(jax.random.key(seed), 2)
    return {
        "trailing": draw_trailing(jax.random.fold_in(seeds[1], 71), 0),
    }


def reference(trailing):
    order_total = NBLK * PANEL
    matrix = trailing.reshape(order_total, order_total)
    for step in range(PANELS):
        start = step * PANEL
        stop = start + PANEL
        lower = jnp.linalg.cholesky(matrix[start:stop, start:stop])
        solved = jax.scipy.linalg.solve_triangular(lower, matrix[stop:, start:stop].T, lower=True).T
        rounded = lax.optimization_barrier(solved.astype(jnp.bfloat16)).astype(jnp.float32)
        update = jnp.dot(rounded, rounded.T, precision=lax.Precision.HIGHEST)
        matrix = matrix.at[stop:, stop:].add(-update)
        matrix = matrix.at[start:stop, start:].set(0.0)
        matrix = matrix.at[start:stop, start:stop].set(lower)
        matrix = matrix.at[stop:, start:stop].set(solved)
    return matrix.reshape(trailing.shape)
```

```python
import functools

import jax
import jax.numpy as jnp
from jax import lax
from jax.experimental import pallas as pl
from jax.experimental.pallas import tpu as pltpu
from jax.sharding import PartitionSpec as P

MESH = pl.DeviceIdType.MESH
HIGHEST = lax.Precision.HIGHEST
OUTER = 64
STRIP = 8
CHUNKS = 4


def dot(a, b, dims, precision=None):
    return lax.dot_general(
        a, b, (dims, ((), ())), precision=precision, preferred_element_type=jnp.float32
    )


def eliminate_block(work, start, width):
    tile = (start // 128) * 128

    def strip(s, carry):
        j0 = pl.multiple_of(start + s * STRIP, STRIP)
        rows = work[pl.ds(j0, STRIP), :]
        near = rows[:, tile:tile + 128]
        lane = lax.broadcasted_iota(jnp.int32, (STRIP, 128), 1) + tile
        sub = lax.broadcasted_iota(jnp.int32, (STRIP, 1), 0)
        cols = [
            jnp.sum(jnp.where(lane == j0 + k, near, 0.0), axis=1, keepdims=True)
            for k in range(STRIP)
        ]
        for k in range(STRIP):
            pivot = cols[k][k:k + 1]
            inv = lax.rsqrt(pivot)
            inv = inv * (1.5 - 0.5 * pivot * inv * inv)
            mult = cols[k] * inv
            for m in range(k + 1, STRIP):
                cols[m] = cols[m] - mult * mult[m:m + 1]
            row = rows[k:k + 1] * inv
            rows = jnp.where(sub == k, row, jnp.where(sub > k, rows - mult * row, rows))
        work[pl.ds(j0, STRIP), :] = rows
        here = lax.broadcasted_iota(jnp.int32, (STRIP, OUTER), 1)
        left = jnp.where(here >= (s + 1) * STRIP, rows[:, start:start + OUTER], 0.0)
        work[start:start + OUTER, :] -= dot(left, rows, ((0,), (0,)), HIGHEST)
        return carry

    lax.fori_loop(0, OUTER // STRIP, strip, 0)
    stop = start + OUTER
    if stop < width:
        done = work[start:stop, :]
        work[stop:width, :] -= dot(done[:, stop:width], done, ((0,), (0,)), HIGHEST)


def load_work(work, block, width):
    work[:, :width] = block
    r = lax.broadcasted_iota(jnp.int32, (width, width), 0)
    c = lax.broadcasted_iota(jnp.int32, (width, width), 1)
    work[:, width:] = jnp.where(r == c, 1.0, 0.0)


def panel_kernel(n_row, n_col, width, col_blocks, local, x_out, u_out, b01_out, bcol, brow,
                 strips, diag, work, local_sem, d_send, d_recv, d_csend, s_send, s_recv,
                 b_send, b_recv):
    r = lax.axis_index("row")
    c = lax.axis_index("col")
    n_z = n_col // 2
    z = c // 2
    core = lax.rem(c, 2)
    ratio = n_col // n_row
    tiles = col_blocks * width // 128
    per = width // 128
    strip_rows = width * tiles

    barrier = pltpu.get_barrier_semaphore()
    for step in range(1, n_row):
        pl.semaphore_signal(barrier, inc=1, device_id=(lax.rem(r + step, n_row), c),
                            device_id_type=MESH)
    pl.semaphore_signal(barrier, inc=1, device_id=(r, z * 2 + 1 - core), device_id_type=MESH)

    @pl.when(z < n_z - 1)
    def _():
        pl.semaphore_signal(barrier, inc=1, device_id=(r, c + 2), device_id_type=MESH)

    @pl.when(z > 0)
    def _():
        pl.semaphore_signal(barrier, inc=1, device_id=(r, c - 2), device_id_type=MESH)

    own = pltpu.make_async_copy(local.at[pl.ds(0, strip_rows)], strips.at[lax.rem(r, 2)],
                                local_sem)

    @pl.when(r < 2)
    def _():
        own.start()

    pl.semaphore_wait(barrier, n_row + jnp.where(z < n_z - 1, 1, 0) + jnp.where(z > 0, 1, 0))

    @pl.when(r < 2)
    def _():
        own.wait()

    owners = ((0, 0), (0, 1), (1, 1))

    def diag_copy(x, step):
        return pltpu.make_async_remote_copy(
            src_ref=diag.at[x], dst_ref=diag.at[x], send_sem=d_send.at[x, step - 1],
            recv_sem=d_recv.at[x], device_id=(lax.rem(r + step, n_row), c), device_id_type=MESH)

    for x, (k, cc) in enumerate(owners):
        @pl.when((r == k) & (c == cc))
        def _(x=x, k=k):
            for h in range(per):
                diag[x, :, h * 128:(h + 1) * 128] = strips[k, pl.ds(h, width, stride=tiles), :]
            for step in range(1, n_row):
                diag_copy(x, step).start()

    def strip_copy(k, step):
        return pltpu.make_async_remote_copy(
            src_ref=strips.at[k], dst_ref=strips.at[k], send_sem=s_send.at[k, step - 1],
            recv_sem=s_recv.at[k], device_id=(lax.rem(r + step, n_row), c), device_id_type=MESH)

    def chain(src, send, recv, zs, lane, extra_source):
        def to(i, cc):
            return pltpu.make_async_remote_copy(
                src_ref=src, dst_ref=src, send_sem=send(i), recv_sem=recv,
                device_id=(r, cc), device_id_type=MESH)
        on_lane = core == lane
        up = on_lane & (z >= zs) & (z < n_z - 1)
        down = on_lane & (z <= zs) & (z > 0)
        others = ((0, up, jnp.minimum(c + 2, n_col - 1)), (1, down, jnp.maximum(c - 2, 0)),
                  (2, on_lane, z * 2 + 1 - core))

        def begin():
            @pl.when(jnp.logical_not(on_lane & (z == zs) & extra_source))
            def _():
                to(2, z * 2 + 1 - core).wait_recv()
            for i, cond, cc in others:
                @pl.when(cond)
                def _(i=i, cc=cc):
                    to(i, cc).start()

        def end():
            for i, cond, cc in others:
                @pl.when(cond)
                def _(i=i, cc=cc):
                    to(i, cc).wait_send()
        return begin, end

    ends = []

    def run_chain(*args):
        begin, end = chain(*args)
        begin()
        ends.append(end)

    def diag_chain(x):
        k, cc = owners[x]
        run_chain(diag.at[x], lambda i: d_csend.at[x, i], d_recv.at[x], 0, cc % 2, r == k)

    diag_chain(0)

    for k in range(2):
        @pl.when(r == k)
        def _(k=k):
            for step in range(1, n_row):
                strip_copy(k, step).start()

    piece = width // CHUNKS

    def panel_chain(k, q):
        for s in range(ratio):
            run_chain(brow.at[2 * s + k, pl.ds(q * piece, piece)],
                      lambda i, s=s: b_send.at[s, k, q, i], b_recv.at[s, k, q],
                      (r + n_row * s) // 2, lax.rem(r, 2), True)

    def need_strip(k):
        @pl.when(r != k)
        def _():
            strip_copy(k, 1).wait_recv()

    def keep_source(k):
        for s in range(ratio):
            @pl.when(c == r + n_row * s)
            def _(s=s):
                brow[2 * s + k] = bcol[k]

    def strip_tile(k, t):
        return jnp.concatenate(
            [strips[k, pl.ds(t * per + h, width, stride=tiles), :] for h in range(per)], axis=1)

    def finish(k):
        rr = lax.broadcasted_iota(jnp.int32, (width, width), 0)
        cc = lax.broadcasted_iota(jnp.int32, (width, width), 1)
        u_out[k] = jnp.where(cc >= rr, work[:, :width], 0.0)
        x_out[k] = jnp.where(cc <= rr, work[:, width:], 0.0)

    load_work(work, diag[0], width)
    for start in range(0, width, OUTER):
        eliminate_block(work, start, width)
        if start == 0:
            diag_chain(1)
        if start == OUTER:
            diag_chain(2)
    finish(0)
    b01 = dot(x_out[0], diag[1], ((1,), (0,)), HIGHEST).astype(jnp.bfloat16)
    b01_out[...] = b01
    need_strip(0)
    for t in range(col_blocks):
        bcol[0, :, t * width:(t + 1) * width] = dot(
            x_out[0], strip_tile(0, t), ((1,), (0,)), HIGHEST).astype(jnp.bfloat16)
    keep_source(0)
    load_work(work, diag[2] - dot(b01, b01, ((0,), (0,))), width)
    every = max(1, (width // OUTER) // CHUNKS)
    queue = list(range(CHUNKS))
    for start in range(0, width, OUTER):
        panel_chain(0, queue.pop(0))
        eliminate_block(work, start, width)
    for q in queue:
        panel_chain(0, q)
    finish(1)
    need_strip(1)
    for t in range(col_blocks):
        at = slice(t * width, (t + 1) * width)
        rest = strip_tile(1, t) - dot(b01_out[...], bcol[0, :, at], ((0,), (0,)))
        bcol[1, :, at] = dot(x_out[1], rest, ((1,), (0,)), HIGHEST).astype(jnp.bfloat16)
    keep_source(1)
    for q in range(CHUNKS):
        panel_chain(1, q)

    for end in ends:
        end()
    for x, (k, cc) in enumerate(owners):
        @pl.when((r == k) & (c == cc))
        def _(x=x):
            for step in range(1, n_row):
                diag_copy(x, step).wait_send()
    for k in range(2):
        @pl.when(r == k)
        def _(k=k):
            for step in range(1, n_row):
                strip_copy(k, step).wait_send()


def update_kernel(n_row, n_col, width, col_blocks, place, m_ref, brow, bcol, x_ref, u_ref, b01,
                  out_ref):
    rb = pl.program_id(0)
    r = place[0]
    c = place[1]
    tiles = col_blocks * width // 128
    per = width // 128
    left = brow[...].reshape(2 * width, width)
    right = bcol[...].reshape(2 * width, col_blocks * width)
    for t in range(col_blocks):
        new = dot(left, right[:, t * width:(t + 1) * width], ((0,), (0,)))
        for h in range(per):
            at = pl.ds(t * per + h, width, stride=tiles)
            out_ref[at, :] = m_ref[at, :] - new[:, h * 128:(h + 1) * 128]

    top = (rb == 0) & (r < 2)

    @pl.when(top)
    def _():
        out_ref[...] = jnp.zeros_like(out_ref)

    def put(block):
        for h in range(per):
            out_ref[pl.ds(h, width, stride=tiles), :] = block[:, h * 128:(h + 1) * 128]

    def get():
        return jnp.concatenate(
            [m_ref[pl.ds(h, width, stride=tiles), :] for h in range(per)], axis=1)

    @pl.when((c == 0) & jnp.logical_not((rb == 0) & (r == 0)))
    def _():
        put(dot(get(), x_ref[0], ((1,), (1,)), HIGHEST))

    @pl.when((c == 1) & jnp.logical_not(top))
    def _():
        rest = get() - dot(left[:width], b01[...], ((0,), (0,)))
        put(dot(rest, x_ref[1], ((1,), (1,)), HIGHEST))

    @pl.when((rb == 0) & (r == c) & (r < 2))
    def _():
        put(jnp.where(r == 0, u_ref[0], u_ref[1]).T)


def body(n_row, n_col, trailing):
    shape = trailing.shape
    row_blocks, width, col_blocks = shape[0], shape[2], shape[3]
    ratio = n_col // n_row
    tiles = col_blocks * width // 128
    block_rows = width * tiles
    local = trailing.reshape(row_blocks * block_rows, 128)
    wide = col_blocks * width
    vmem = pl.BlockSpec(memory_space=pltpu.VMEM)
    x_f, u_f, b01, bcol, brow = pl.pallas_call(
        functools.partial(panel_kernel, n_row, n_col, width, col_blocks),
        out_shape=(
            jax.ShapeDtypeStruct((2, width, width), jnp.float32),
            jax.ShapeDtypeStruct((2, width, width), jnp.float32),
            jax.ShapeDtypeStruct((width, width), jnp.bfloat16),
            jax.ShapeDtypeStruct((2, width, wide), jnp.bfloat16),
            jax.ShapeDtypeStruct((2 * ratio, width, wide), jnp.bfloat16),
        ),
        in_specs=[pl.BlockSpec(memory_space=pl.ANY)],
        out_specs=(vmem,) * 5,
        scratch_shapes=[
            pltpu.VMEM((2, block_rows, 128), jnp.float32),
            pltpu.VMEM((3, width, width), jnp.float32),
            pltpu.VMEM((width, 2 * width), jnp.float32),
            pltpu.SemaphoreType.DMA,
            pltpu.SemaphoreType.DMA((3, n_row - 1)),
            pltpu.SemaphoreType.DMA((3,)),
            pltpu.SemaphoreType.DMA((3, 3)),
            pltpu.SemaphoreType.DMA((2, n_row - 1)),
            pltpu.SemaphoreType.DMA((2,)),
            pltpu.SemaphoreType.DMA((ratio, 2, CHUNKS, 3)),
            pltpu.SemaphoreType.DMA((ratio, 2, CHUNKS)),
        ],
        compiler_params=pltpu.CompilerParams(
            collective_id=0, has_side_effects=True, vmem_limit_bytes=48 * 1024 * 1024),
        name="panels",
    )(local)
    place = jnp.stack([lax.axis_index("row"), lax.axis_index("col")]).astype(jnp.int32)
    out = pl.pallas_call(
        functools.partial(update_kernel, n_row, n_col, width, col_blocks),
        grid_spec=pltpu.PrefetchScalarGridSpec(
            num_scalar_prefetch=1,
            grid=(row_blocks,),
            in_specs=[
                pl.BlockSpec((block_rows, 128), lambda i, p: (i, 0)),
                pl.BlockSpec((2, width, width), lambda i, p: (i % ratio, 0, i // ratio)),
                pl.BlockSpec((2, width, wide), lambda i, p: (0, 0, 0)),
                pl.BlockSpec((2, width, width), lambda i, p: (0, 0, 0)),
                pl.BlockSpec((2, width, width), lambda i, p: (0, 0, 0)),
                pl.BlockSpec((width, width), lambda i, p: (0, 0)),
            ],
            out_specs=pl.BlockSpec((block_rows, 128), lambda i, p: (i, 0)),
        ),
        out_shape=jax.ShapeDtypeStruct(local.shape, jnp.float32),
        compiler_params=pltpu.CompilerParams(vmem_limit_bytes=48 * 1024 * 1024),
        name="update",
    )(place, local, brow, bcol, x_f, u_f, b01)
    return out.reshape(shape)


def solution(mesh):
    placed = P(None, "row", None, None, "col", None)
    return jax.shard_map(
        functools.partial(body, mesh.shape["row"], mesh.shape["col"]),
        mesh=mesh,
        in_specs=(placed,),
        out_specs=placed,
        check_vma=False,
    )
```

```python
import functools

import jax
import jax.numpy as jnp
from jax import lax
from jax.experimental import pallas as pl
from jax.experimental.pallas import tpu as pltpu
from jax.sharding import PartitionSpec as P

MESH = pl.DeviceIdType.MESH
HIGHEST = lax.Precision.HIGHEST
OUTER = 64
STRIP = 8
PARTS = 4


def dot(a, b, dims, precision=None):
    return lax.dot_general(
        a, b, (dims, ((), ())), precision=precision, preferred_element_type=jnp.float32
    )


def eliminate_block(work, start, width):
    tile = (start // 128) * 128

    def strip(s, carry):
        j0 = pl.multiple_of(start + s * STRIP, STRIP)
        rows = work[pl.ds(j0, STRIP), :]
        near = rows[:, tile:tile + 128]
        lane = lax.broadcasted_iota(jnp.int32, (STRIP, 128), 1) + tile
        sub = lax.broadcasted_iota(jnp.int32, (STRIP, 1), 0)
        cols = [
            jnp.sum(jnp.where(lane == j0 + k, near, 0.0), axis=1, keepdims=True)
            for k in range(STRIP)
        ]
        for k in range(STRIP):
            pivot = cols[k][k:k + 1]
            inv = lax.rsqrt(pivot)
            inv = inv * (1.5 - 0.5 * pivot * inv * inv)
            mult = cols[k] * inv
            for m in range(k + 1, STRIP):
                cols[m] = cols[m] - mult * mult[m:m + 1]
            row = rows[k:k + 1] * inv
            rows = jnp.where(sub == k, row, jnp.where(sub > k, rows - mult * row, rows))
        work[pl.ds(j0, STRIP), :] = rows
        here = lax.broadcasted_iota(jnp.int32, (STRIP, OUTER), 1)
        left = jnp.where(here >= (s + 1) * STRIP, rows[:, start:start + OUTER], 0.0)
        work[start:start + OUTER, :] -= dot(left, rows, ((0,), (0,)), HIGHEST)
        return carry

    lax.fori_loop(0, OUTER // STRIP, strip, 0)
    stop = start + OUTER
    if stop < width:
        done = work[start:stop, :]
        work[stop:width, :] -= dot(done[:, stop:width], done, ((0,), (0,)), HIGHEST)


def load_work(work, block, width):
    work[:, :width] = block
    r = lax.broadcasted_iota(jnp.int32, (width, width), 0)
    c = lax.broadcasted_iota(jnp.int32, (width, width), 1)
    work[:, width:] = jnp.where(r == c, 1.0, 0.0)


def panel_kernel(n_row, n_col, width, col_blocks, local, x_out, u_out, b01_out, bcol, brow,
                 strips, diag, work, local_sem, d_send, d_recv, d_csend, s_send, s_recv,
                 b_send, b_recv):
    r = lax.axis_index("row")
    c = lax.axis_index("col")
    n_z = n_col // 2
    z = c // 2
    core = lax.rem(c, 2)
    ratio = n_col // n_row
    tiles = col_blocks * width // 128
    per = width // 128
    strip_rows = width * tiles

    barrier = pltpu.get_barrier_semaphore()
    for step in range(1, n_row):
        pl.semaphore_signal(barrier, inc=1, device_id=(lax.rem(r + step, n_row), c),
                            device_id_type=MESH)
    pl.semaphore_signal(barrier, inc=1, device_id=(r, z * 2 + 1 - core), device_id_type=MESH)

    @pl.when(z < n_z - 1)
    def _():
        pl.semaphore_signal(barrier, inc=1, device_id=(r, c + 2), device_id_type=MESH)

    @pl.when(z > 0)
    def _():
        pl.semaphore_signal(barrier, inc=1, device_id=(r, c - 2), device_id_type=MESH)

    own = pltpu.make_async_copy(local.at[pl.ds(0, strip_rows)], strips.at[lax.rem(r, 2)],
                                local_sem)

    @pl.when(r < 2)
    def _():
        own.start()

    pl.semaphore_wait(barrier, n_row + jnp.where(z < n_z - 1, 1, 0) + jnp.where(z > 0, 1, 0))

    @pl.when(r < 2)
    def _():
        own.wait()

    owners = ((0, 0), (0, 1), (1, 1))
    part = width // PARTS
    blocks = width // OUTER

    def diag_piece(x, p):
        return diag.at[x, pl.ds(p * part, part)]

    def diag_copy(x, p, step):
        return pltpu.make_async_remote_copy(
            src_ref=diag_piece(x, p), dst_ref=diag_piece(x, p),
            send_sem=d_send.at[x, p, step - 1], recv_sem=d_recv.at[x, p],
            device_id=(lax.rem(r + step, n_row), c), device_id_type=MESH)

    def diag_start(x):
        k, cc = owners[x]

        @pl.when((r == k) & (c == cc))
        def _():
            for h in range(per):
                diag[x, :, h * 128:(h + 1) * 128] = strips[k, pl.ds(h, width, stride=tiles), :]
            for p in range(PARTS):
                for step in range(1, n_row):
                    diag_copy(x, p, step).start()

    half = strip_rows // PARTS
    buddy = r + 1 - 2 * lax.rem(r, 2)

    def strip_copy(k, p, i, target):
        piece = strips.at[k, pl.ds(p * half, half)]
        return pltpu.make_async_remote_copy(
            src_ref=piece, dst_ref=piece, send_sem=s_send.at[k, p, i],
            recv_sem=s_recv.at[k, p], device_id=(target, c), device_id_type=MESH)

    def strip_start():
        for k in range(2):
            @pl.when(r == k)
            def _(k=k):
                for p in range(PARTS):
                    for i in range(1, n_row // 2):
                        strip_copy(k, p, i, k + 2 * i).start()
                    strip_copy(k, p, 0, buddy).start()

    def strip_relay(p):
        for k in range(2):
            @pl.when((r != k) & (lax.rem(r, 2) == k))
            def _(k=k):
                strip_copy(k, p, 0, buddy).wait_recv()
                strip_copy(k, p, 0, buddy).start()

    def strip_need(k):
        @pl.when(lax.rem(r, 2) != k)
        def _():
            for p in range(PARTS):
                strip_copy(k, p, 0, buddy).wait_recv()

    def chain(src, send, recv, zs, lane):
        def to(i, cc):
            return pltpu.make_async_remote_copy(
                src_ref=src, dst_ref=src, send_sem=send(i), recv_sem=recv,
                device_id=(r, cc), device_id_type=MESH)
        on_lane = core == lane
        up = on_lane & (z >= zs) & (z < n_z - 1)
        down = on_lane & (z <= zs) & (z > 0)
        links = ((0, up, jnp.minimum(c + 2, n_col - 1)), (1, down, jnp.maximum(c - 2, 0)),
                 (2, on_lane, z * 2 + 1 - core))

        def receive():
            to(2, z * 2 + 1 - core).wait_recv()

        def send_on():
            for i, cond, cc in links:
                @pl.when(cond)
                def _(i=i, cc=cc):
                    to(i, cc).start()

        def end():
            for i, cond, cc in links:
                @pl.when(cond)
                def _(i=i, cc=cc):
                    to(i, cc).wait_send()
        return receive, send_on, end

    def diag_link(x, p):
        return chain(diag_piece(x, p), lambda i: d_csend.at[x, p, i], d_recv.at[x, p], 0,
                     owners[x][1] % 2)

    def diag_chain(x):
        k, cc = owners[x]
        for p in range(PARTS):
            receive, send_on, _ = diag_link(x, p)

            @pl.when(jnp.logical_not((r == k) & (c == cc)))
            def _(receive=receive):
                receive()
            send_on()

    def panel_link(s, k, t):
        return chain(brow.at[2 * s + k, :, pl.ds(t * width, width)],
                     lambda i: b_send.at[s, k, t, i], b_recv.at[s, k, t],
                     (r + n_row * s) // 2, lax.rem(r, 2))

    lane_core = core == lax.rem(r, 2)

    def distance(s):
        return jnp.abs(z - (r + n_row * s) // 2)

    def panel_source(k, t):
        for s in range(ratio):
            @pl.when(c == r + n_row * s)
            def _(s=s):
                at = slice(t * width, (t + 1) * width)
                brow[2 * s + k, :, at] = bcol[k, :, at]
                panel_link(s, k, t)[1]()

    def panel_relay(k, t, s, cond):
        @pl.when(cond)
        def _():
            receive, send_on, _ = panel_link(s, k, t)
            receive()
            send_on()

    def strip_tile(k, t):
        return jnp.concatenate(
            [strips[k, pl.ds(t * per + h, width, stride=tiles), :] for h in range(per)], axis=1)

    def finish(k):
        rr = lax.broadcasted_iota(jnp.int32, (width, width), 0)
        cc = lax.broadcasted_iota(jnp.int32, (width, width), 1)
        u_out[k] = jnp.where(cc >= rr, work[:, :width], 0.0)
        x_out[k] = jnp.where(cc <= rr, work[:, width:], 0.0)

    diag_start(0)

    @pl.when(z > 0)
    def _():
        strip_start()

    diag_chain(0)
    load_work(work, diag[0], width)
    for b in range(blocks):
        eliminate_block(work, b * OUTER, width)
        if b == 0:
            diag_start(1)
            diag_start(2)

            @pl.when(z == 0)
            def _():
                strip_start()
        if b == 1:
            strip_relay(0)
        if b == 2:
            strip_relay(1)
            diag_chain(1)
        if b == 3:
            strip_relay(2)
            diag_chain(2)
    finish(0)
    b01 = dot(x_out[0], diag[1], ((1,), (0,)), HIGHEST).astype(jnp.bfloat16)
    b01_out[...] = b01
    strip_relay(3)
    strip_need(0)
    for t in range(col_blocks):
        bcol[0, :, t * width:(t + 1) * width] = dot(
            x_out[0], strip_tile(0, t), ((1,), (0,)), HIGHEST).astype(jnp.bfloat16)
        panel_source(0, t)
    load_work(work, diag[2] - dot(b01, b01, ((0,), (0,))), width)
    for b in range(blocks):
        eliminate_block(work, b * OUTER, width)
        for s in range(ratio):
            far = distance(s) >= b + 1 if b == blocks - 1 else distance(s) == b + 1
            for t in range(col_blocks):
                panel_relay(0, t, s, lane_core & far)
    finish(1)
    strip_need(1)
    for t in range(col_blocks):
        at = slice(t * width, (t + 1) * width)
        rest = strip_tile(1, t) - dot(b01_out[...], bcol[0, :, at], ((0,), (0,)))
        bcol[1, :, at] = dot(x_out[1], rest, ((1,), (0,)), HIGHEST).astype(jnp.bfloat16)
        panel_source(1, t)
    for t in range(col_blocks):
        for s in range(ratio):
            panel_relay(0, t, s, jnp.logical_not(lane_core))
            panel_relay(1, t, s, jnp.logical_not(lane_core & (distance(s) == 0)))

    for x, (k, cc) in enumerate(owners):
        for p in range(PARTS):
            diag_link(x, p)[2]()

            @pl.when((r == k) & (c == cc))
            def _(x=x, p=p):
                for step in range(1, n_row):
                    diag_copy(x, p, step).wait_send()
    for k in range(2):
        @pl.when(lax.rem(r, 2) == k)
        def _(k=k):
            for p in range(PARTS):
                strip_copy(k, p, 0, buddy).wait_send()

        @pl.when(r == k)
        def _(k=k):
            for p in range(PARTS):
                for i in range(1, n_row // 2):
                    strip_copy(k, p, i, k + 2 * i).wait_send()
    for s in range(ratio):
        for k in range(2):
            for t in range(col_blocks):
                panel_link(s, k, t)[2]()


def update_kernel(n_row, n_col, width, col_blocks, place, m_ref, brow, bcol, x_ref, u_ref, b01,
                  out_ref):
    rb = pl.program_id(0)
    r = place[0]
    c = place[1]
    tiles = col_blocks * width // 128
    per = width // 128
    left = brow[...].reshape(2 * width, width)
    right = bcol[...].reshape(2 * width, col_blocks * width)
    for t in range(col_blocks):
        new = dot(left, right[:, t * width:(t + 1) * width], ((0,), (0,)))
        for h in range(per):
            at = pl.ds(t * per + h, width, stride=tiles)
            out_ref[at, :] = m_ref[at, :] - new[:, h * 128:(h + 1) * 128]

    top = (rb == 0) & (r < 2)

    @pl.when(top)
    def _():
        out_ref[...] = jnp.zeros_like(out_ref)

    def put(block):
        for h in range(per):
            out_ref[pl.ds(h, width, stride=tiles), :] = block[:, h * 128:(h + 1) * 128]

    def get():
        return jnp.concatenate(
            [m_ref[pl.ds(h, width, stride=tiles), :] for h in range(per)], axis=1)

    @pl.when((c == 0) & jnp.logical_not((rb == 0) & (r == 0)))
    def _():
        put(dot(get(), x_ref[0], ((1,), (1,)), HIGHEST))

    @pl.when((c == 1) & jnp.logical_not(top))
    def _():
        rest = get() - dot(left[:width], b01[...], ((0,), (0,)))
        put(dot(rest, x_ref[1], ((1,), (1,)), HIGHEST))

    @pl.when((rb == 0) & (r == c) & (r < 2))
    def _():
        put(jnp.where(r == 0, u_ref[0], u_ref[1]).T)


def body(n_row, n_col, trailing):
    shape = trailing.shape
    row_blocks, width, col_blocks = shape[0], shape[2], shape[3]
    ratio = n_col // n_row
    tiles = col_blocks * width // 128
    block_rows = width * tiles
    local = trailing.reshape(row_blocks * block_rows, 128)
    wide = col_blocks * width
    vmem = pl.BlockSpec(memory_space=pltpu.VMEM)
    x_f, u_f, b01, bcol, brow = pl.pallas_call(
        functools.partial(panel_kernel, n_row, n_col, width, col_blocks),
        out_shape=(
            jax.ShapeDtypeStruct((2, width, width), jnp.float32),
            jax.ShapeDtypeStruct((2, width, width), jnp.float32),
            jax.ShapeDtypeStruct((width, width), jnp.bfloat16),
            jax.ShapeDtypeStruct((2, width, wide), jnp.bfloat16),
            jax.ShapeDtypeStruct((2 * ratio, width, wide), jnp.bfloat16),
        ),
        in_specs=[pl.BlockSpec(memory_space=pl.ANY)],
        out_specs=(vmem,) * 5,
        scratch_shapes=[
            pltpu.VMEM((2, block_rows, 128), jnp.float32),
            pltpu.VMEM((3, width, width), jnp.float32),
            pltpu.VMEM((width, 2 * width), jnp.float32),
            pltpu.SemaphoreType.DMA,
            pltpu.SemaphoreType.DMA((3, PARTS, n_row - 1)),
            pltpu.SemaphoreType.DMA((3, PARTS)),
            pltpu.SemaphoreType.DMA((3, PARTS, 3)),
            pltpu.SemaphoreType.DMA((2, PARTS, n_row // 2)),
            pltpu.SemaphoreType.DMA((2, PARTS)),
            pltpu.SemaphoreType.DMA((ratio, 2, col_blocks, 3)),
            pltpu.SemaphoreType.DMA((ratio, 2, col_blocks)),
        ],
        compiler_params=pltpu.CompilerParams(
            collective_id=0, has_side_effects=True, vmem_limit_bytes=48 * 1024 * 1024),
        name="panels",
    )(local)
    place = jnp.stack([lax.axis_index("row"), lax.axis_index("col")]).astype(jnp.int32)
    out = pl.pallas_call(
        functools.partial(update_kernel, n_row, n_col, width, col_blocks),
        grid_spec=pltpu.PrefetchScalarGridSpec(
            num_scalar_prefetch=1,
            grid=(row_blocks,),
            in_specs=[
                pl.BlockSpec((block_rows, 128), lambda i, p: (i, 0)),
                pl.BlockSpec((2, width, width), lambda i, p: (i % ratio, 0, i // ratio)),
                pl.BlockSpec((2, width, wide), lambda i, p: (0, 0, 0)),
                pl.BlockSpec((2, width, width), lambda i, p: (0, 0, 0)),
                pl.BlockSpec((2, width, width), lambda i, p: (0, 0, 0)),
                pl.BlockSpec((width, width), lambda i, p: (0, 0)),
            ],
            out_specs=pl.BlockSpec((block_rows, 128), lambda i, p: (i, 0)),
        ),
        out_shape=jax.ShapeDtypeStruct(local.shape, jnp.float32),
        compiler_params=pltpu.CompilerParams(vmem_limit_bytes=48 * 1024 * 1024),
        name="update",
    )(place, local, brow, bcol, x_f, u_f, b01)
    return out.reshape(shape)


def solution(mesh):
    placed = P(None, "row", None, None, "col", None)
    return jax.shard_map(
        functools.partial(body, mesh.shape["row"], mesh.shape["col"]),
        mesh=mesh,
        in_specs=(placed,),
        out_specs=placed,
        check_vma=False,
    )
```

```python
import functools

import jax
import jax.numpy as jnp
from jax import lax
from jax.experimental import pallas as pl
from jax.experimental.pallas import tpu as pltpu
from jax.sharding import PartitionSpec as P

MESH = pl.DeviceIdType.MESH
HIGHEST = lax.Precision.HIGHEST
OUTER = 64
STRIP = 8
PARTS = 4


def dot(a, b, dims, precision=None):
    return lax.dot_general(
        a, b, (dims, ((), ())), precision=precision, preferred_element_type=jnp.float32
    )


def eliminate_block(work, start, width):
    stop = start + OUTER
    tile = (start // 128) * 128
    edge = width + -(-stop // 128) * 128
    first = start - tile

    def strip(s, carry):
        j0 = pl.multiple_of(start + s * STRIP, STRIP)
        rows = work[pl.ds(j0, STRIP), tile:edge]
        near = rows[:, :128]
        lane = lax.broadcasted_iota(jnp.int32, (STRIP, 128), 1) + tile
        sub = lax.broadcasted_iota(jnp.int32, (STRIP, 1), 0)
        cols = [
            jnp.sum(jnp.where(lane == j0 + k, near, 0.0), axis=1, keepdims=True)
            for k in range(STRIP)
        ]
        for k in range(STRIP):
            pivot = cols[k][k:k + 1]
            inv = lax.rsqrt(pivot)
            inv = inv * (1.5 - 0.5 * pivot * inv * inv)
            mult = cols[k] * inv
            for m in range(k + 1, STRIP):
                cols[m] = cols[m] - mult * mult[m:m + 1]
            row = rows[k:k + 1] * inv
            rows = jnp.where(sub == k, row, jnp.where(sub > k, rows - mult * row, rows))
        work[pl.ds(j0, STRIP), tile:edge] = rows
        here = lax.broadcasted_iota(jnp.int32, (STRIP, OUTER), 1)
        left = jnp.where(here >= (s + 1) * STRIP, rows[:, first:first + OUTER], 0.0)
        work[start:stop, tile:edge] -= dot(left, rows, ((0,), (0,)), HIGHEST)
        return carry

    lax.fori_loop(0, OUTER // STRIP, strip, 0)
    if stop < width:
        done = work[start:stop, tile:edge]
        work[stop:width, tile:edge] -= dot(done[:, stop - tile:width - tile], done, ((0,), (0,)), HIGHEST)


def load_work(work, block, width):
    work[:, :width] = block
    r = lax.broadcasted_iota(jnp.int32, (width, width), 0)
    c = lax.broadcasted_iota(jnp.int32, (width, width), 1)
    work[:, width:] = jnp.where(r == c, 1.0, 0.0)


def panel_kernel(n_row, n_col, width, col_blocks, local, x_out, u_out, b01_out, bcol, brow,
                 strips, diag, work, local_sem, d_send, d_recv, d_csend, s_send, s_recv,
                 b_send, b_recv):
    r = lax.axis_index("row")
    c = lax.axis_index("col")
    n_z = n_col // 2
    z = c // 2
    core = lax.rem(c, 2)
    ratio = n_col // n_row
    tiles = col_blocks * width // 128
    per = width // 128
    strip_rows = width * tiles

    barrier = pltpu.get_barrier_semaphore()
    for step in range(1, n_row):
        pl.semaphore_signal(barrier, inc=1, device_id=(lax.rem(r + step, n_row), c),
                            device_id_type=MESH)
    pl.semaphore_signal(barrier, inc=1, device_id=(r, z * 2 + 1 - core), device_id_type=MESH)

    @pl.when(z < n_z - 1)
    def _():
        pl.semaphore_signal(barrier, inc=1, device_id=(r, c + 2), device_id_type=MESH)

    @pl.when(z > 0)
    def _():
        pl.semaphore_signal(barrier, inc=1, device_id=(r, c - 2), device_id_type=MESH)

    own = pltpu.make_async_copy(local.at[pl.ds(0, strip_rows)], strips.at[lax.rem(r, 2)],
                                local_sem)

    @pl.when(r < 2)
    def _():
        own.start()

    pl.semaphore_wait(barrier, n_row + jnp.where(z < n_z - 1, 1, 0) + jnp.where(z > 0, 1, 0))

    @pl.when(r < 2)
    def _():
        own.wait()

    owners = ((0, 0), (0, 1), (1, 1))
    part = width // PARTS
    blocks = width // OUTER

    def diag_piece(x, p):
        return diag.at[x, pl.ds(p * part, part)]

    def diag_copy(x, p, step):
        return pltpu.make_async_remote_copy(
            src_ref=diag_piece(x, p), dst_ref=diag_piece(x, p),
            send_sem=d_send.at[x, p, step - 1], recv_sem=d_recv.at[x, p],
            device_id=(lax.rem(r + step, n_row), c), device_id_type=MESH)

    def diag_start(x):
        k, cc = owners[x]

        @pl.when((r == k) & (c == cc))
        def _():
            for h in range(per):
                diag[x, :, h * 128:(h + 1) * 128] = strips[k, pl.ds(h, width, stride=tiles), :]
            for p in range(PARTS):
                for step in range(1, n_row):
                    diag_copy(x, p, step).start()

    half = strip_rows // PARTS
    buddy = r + 1 - 2 * lax.rem(r, 2)

    def strip_copy(k, p, i, target):
        piece = strips.at[k, pl.ds(p * half, half)]
        return pltpu.make_async_remote_copy(
            src_ref=piece, dst_ref=piece, send_sem=s_send.at[k, p, i],
            recv_sem=s_recv.at[k, p], device_id=(target, c), device_id_type=MESH)

    def strip_start():
        for k in range(2):
            @pl.when(r == k)
            def _(k=k):
                for p in range(PARTS):
                    for i in range(1, n_row // 2):
                        strip_copy(k, p, i, k + 2 * i).start()
                    strip_copy(k, p, 0, buddy).start()

    def strip_relay(p):
        for k in range(2):
            @pl.when((r != k) & (lax.rem(r, 2) == k))
            def _(k=k):
                strip_copy(k, p, 0, buddy).wait_recv()
                strip_copy(k, p, 0, buddy).start()

    def strip_need(k):
        @pl.when(lax.rem(r, 2) != k)
        def _():
            for p in range(PARTS):
                strip_copy(k, p, 0, buddy).wait_recv()

    def chain(src, send, recv, zs, lane):
        def to(i, cc):
            return pltpu.make_async_remote_copy(
                src_ref=src, dst_ref=src, send_sem=send(i), recv_sem=recv,
                device_id=(r, cc), device_id_type=MESH)
        on_lane = core == lane
        up = on_lane & (z >= zs) & (z < n_z - 1)
        down = on_lane & (z <= zs) & (z > 0)
        links = ((0, up, jnp.minimum(c + 2, n_col - 1)), (1, down, jnp.maximum(c - 2, 0)),
                 (2, on_lane, z * 2 + 1 - core))

        def receive():
            to(2, z * 2 + 1 - core).wait_recv()

        def send_on():
            for i, cond, cc in links:
                @pl.when(cond)
                def _(i=i, cc=cc):
                    to(i, cc).start()

        def end():
            for i, cond, cc in links:
                @pl.when(cond)
                def _(i=i, cc=cc):
                    to(i, cc).wait_send()
        return receive, send_on, end

    def diag_link(x, p):
        return chain(diag_piece(x, p), lambda i: d_csend.at[x, p, i], d_recv.at[x, p], 0,
                     owners[x][1] % 2)

    def diag_chain(x):
        k, cc = owners[x]
        for p in range(PARTS):
            receive, send_on, _ = diag_link(x, p)

            @pl.when(jnp.logical_not((r == k) & (c == cc)))
            def _(receive=receive):
                receive()
            send_on()

    def panel_link(s, k, t):
        return chain(brow.at[2 * s + k, :, pl.ds(t * width, width)],
                     lambda i: b_send.at[s, k, t, i], b_recv.at[s, k, t],
                     (r + n_row * s) // 2, lax.rem(r, 2))

    lane_core = core == lax.rem(r, 2)

    def distance(s):
        return jnp.abs(z - (r + n_row * s) // 2)

    def panel_source(k, t):
        for s in range(ratio):
            @pl.when(c == r + n_row * s)
            def _(s=s):
                at = slice(t * width, (t + 1) * width)
                brow[2 * s + k, :, at] = bcol[k, :, at]
                panel_link(s, k, t)[1]()

    def panel_relay(k, t, s, cond):
        @pl.when(cond)
        def _():
            receive, send_on, _ = panel_link(s, k, t)
            receive()
            send_on()

    def strip_tile(k, t):
        return jnp.concatenate(
            [strips[k, pl.ds(t * per + h, width, stride=tiles), :] for h in range(per)], axis=1)

    def finish(k):
        rr = lax.broadcasted_iota(jnp.int32, (width, width), 0)
        cc = lax.broadcasted_iota(jnp.int32, (width, width), 1)
        u_out[k] = jnp.where(cc >= rr, work[:, :width], 0.0)
        x_out[k] = jnp.where(cc <= rr, work[:, width:], 0.0)

    diag_start(0)

    @pl.when(z > 0)
    def _():
        strip_start()

    diag_chain(0)
    load_work(work, diag[0], width)
    for b in range(blocks):
        eliminate_block(work, b * OUTER, width)
        if b == 0:
            diag_start(1)
            diag_start(2)

            @pl.when(z == 0)
            def _():
                strip_start()
        if b == 1:
            strip_relay(0)
        if b == 2:
            strip_relay(1)
            diag_chain(1)
        if b == 3:
            strip_relay(2)
            diag_chain(2)
    finish(0)
    b01 = dot(x_out[0], diag[1], ((1,), (0,)), HIGHEST).astype(jnp.bfloat16)
    b01_out[...] = b01
    load_work(work, diag[2] - dot(b01, b01, ((0,), (0,))), width)
    for b in range(blocks):
        eliminate_block(work, b * OUTER, width)
        if b == 0:
            strip_relay(3)
        if b == 1:
            strip_need(0)
            for t in range(col_blocks):
                bcol[0, :, t * width:(t + 1) * width] = dot(
                    x_out[0], strip_tile(0, t), ((1,), (0,)), HIGHEST).astype(jnp.bfloat16)
                panel_source(0, t)
        if b >= 2:
            for s in range(ratio):
                for t in range(col_blocks):
                    panel_relay(0, t, s, lane_core & (distance(s) == b - 1))
    finish(1)
    strip_need(1)
    for t in range(col_blocks):
        at = slice(t * width, (t + 1) * width)
        rest = strip_tile(1, t) - dot(b01_out[...], bcol[0, :, at], ((0,), (0,)))
        bcol[1, :, at] = dot(x_out[1], rest, ((1,), (0,)), HIGHEST).astype(jnp.bfloat16)
        panel_source(1, t)
    for t in range(col_blocks):
        for s in range(ratio):
            panel_relay(0, t, s, jnp.logical_not(lane_core & (distance(s) <= blocks - 2)))
            panel_relay(1, t, s, jnp.logical_not(lane_core & (distance(s) == 0)))

    for x, (k, cc) in enumerate(owners):
        for p in range(PARTS):
            diag_link(x, p)[2]()

            @pl.when((r == k) & (c == cc))
            def _(x=x, p=p):
                for step in range(1, n_row):
                    diag_copy(x, p, step).wait_send()
    for k in range(2):
        @pl.when(lax.rem(r, 2) == k)
        def _(k=k):
            for p in range(PARTS):
                strip_copy(k, p, 0, buddy).wait_send()

        @pl.when(r == k)
        def _(k=k):
            for p in range(PARTS):
                for i in range(1, n_row // 2):
                    strip_copy(k, p, i, k + 2 * i).wait_send()
    for s in range(ratio):
        for k in range(2):
            for t in range(col_blocks):
                panel_link(s, k, t)[2]()


def update_kernel(n_row, n_col, width, col_blocks, place, m_ref, brow, bcol, x_ref, u_ref, b01,
                  out_ref):
    rb = pl.program_id(0)
    r = place[0]
    c = place[1]
    tiles = col_blocks * width // 128
    per = width // 128
    left = brow[...].reshape(2 * width, width)
    right = bcol[...].reshape(2 * width, col_blocks * width)
    for t in range(col_blocks):
        new = dot(left, right[:, t * width:(t + 1) * width], ((0,), (0,)))
        for h in range(per):
            at = pl.ds(t * per + h, width, stride=tiles)
            out_ref[at, :] = m_ref[at, :] - new[:, h * 128:(h + 1) * 128]

    top = (rb == 0) & (r < 2)

    @pl.when(top)
    def _():
        out_ref[...] = jnp.zeros_like(out_ref)

    def put(block):
        for h in range(per):
            out_ref[pl.ds(h, width, stride=tiles), :] = block[:, h * 128:(h + 1) * 128]

    def get():
        return jnp.concatenate(
            [m_ref[pl.ds(h, width, stride=tiles), :] for h in range(per)], axis=1)

    @pl.when((c == 0) & jnp.logical_not((rb == 0) & (r == 0)))
    def _():
        put(dot(get(), x_ref[0], ((1,), (1,)), HIGHEST))

    @pl.when((c == 1) & jnp.logical_not(top))
    def _():
        rest = get() - dot(left[:width], b01[...], ((0,), (0,)))
        put(dot(rest, x_ref[1], ((1,), (1,)), HIGHEST))

    @pl.when((rb == 0) & (r == c) & (r < 2))
    def _():
        put(jnp.where(r == 0, u_ref[0], u_ref[1]).T)


def body(n_row, n_col, trailing):
    shape = trailing.shape
    row_blocks, width, col_blocks = shape[0], shape[2], shape[3]
    ratio = n_col // n_row
    tiles = col_blocks * width // 128
    block_rows = width * tiles
    local = trailing.reshape(row_blocks * block_rows, 128)
    wide = col_blocks * width
    vmem = pl.BlockSpec(memory_space=pltpu.VMEM)
    x_f, u_f, b01, bcol, brow = pl.pallas_call(
        functools.partial(panel_kernel, n_row, n_col, width, col_blocks),
        out_shape=(
            jax.ShapeDtypeStruct((2, width, width), jnp.float32),
            jax.ShapeDtypeStruct((2, width, width), jnp.float32),
            jax.ShapeDtypeStruct((width, width), jnp.bfloat16),
            jax.ShapeDtypeStruct((2, width, wide), jnp.bfloat16),
            jax.ShapeDtypeStruct((2 * ratio, width, wide), jnp.bfloat16),
        ),
        in_specs=[pl.BlockSpec(memory_space=pl.ANY)],
        out_specs=(vmem,) * 5,
        scratch_shapes=[
            pltpu.VMEM((2, block_rows, 128), jnp.float32),
            pltpu.VMEM((3, width, width), jnp.float32),
            pltpu.VMEM((width, 2 * width), jnp.float32),
            pltpu.SemaphoreType.DMA,
            pltpu.SemaphoreType.DMA((3, PARTS, n_row - 1)),
            pltpu.SemaphoreType.DMA((3, PARTS)),
            pltpu.SemaphoreType.DMA((3, PARTS, 3)),
            pltpu.SemaphoreType.DMA((2, PARTS, n_row // 2)),
            pltpu.SemaphoreType.DMA((2, PARTS)),
            pltpu.SemaphoreType.DMA((ratio, 2, col_blocks, 3)),
            pltpu.SemaphoreType.DMA((ratio, 2, col_blocks)),
        ],
        compiler_params=pltpu.CompilerParams(
            collective_id=0, has_side_effects=True, vmem_limit_bytes=48 * 1024 * 1024),
        name="panels",
    )(local)
    place = jnp.stack([lax.axis_index("row"), lax.axis_index("col")]).astype(jnp.int32)
    out = pl.pallas_call(
        functools.partial(update_kernel, n_row, n_col, width, col_blocks),
        grid_spec=pltpu.PrefetchScalarGridSpec(
            num_scalar_prefetch=1,
            grid=(row_blocks,),
            in_specs=[
                pl.BlockSpec((block_rows, 128), lambda i, p: (i, 0)),
                pl.BlockSpec((2, width, width), lambda i, p: (i % ratio, 0, i // ratio)),
                pl.BlockSpec((2, width, wide), lambda i, p: (0, 0, 0)),
                pl.BlockSpec((2, width, width), lambda i, p: (0, 0, 0)),
                pl.BlockSpec((2, width, width), lambda i, p: (0, 0, 0)),
                pl.BlockSpec((width, width), lambda i, p: (0, 0)),
            ],
            out_specs=pl.BlockSpec((block_rows, 128), lambda i, p: (i, 0)),
        ),
        out_shape=jax.ShapeDtypeStruct(local.shape, jnp.float32),
        compiler_params=pltpu.CompilerParams(vmem_limit_bytes=48 * 1024 * 1024),
        name="update",
    )(place, local, brow, bcol, x_f, u_f, b01)
    return out.reshape(shape)


def solution(mesh):
    placed = P(None, "row", None, None, "col", None)
    return jax.shard_map(
        functools.partial(body, mesh.shape["row"], mesh.shape["col"]),
        mesh=mesh,
        in_specs=(placed,),
        out_specs=placed,
        check_vma=False,
    )
```
